32 devices in a mesh: group: 4 (over y, x), inner: 8 (over z, core).
Axes of the slice: x: 2, y: 2, z: 4, core: 2. Of those that a mesh axis runs over, the one named last changes fastest.
Arguments:
- node_feats: bfloat16 [196608, 256], P(('group', 'inner')), may hold values from -6 to 6
- adj_tiles: bfloat16 [196608, 512], P(('group', 'inner')), may hold values from -0.25 to 0.25
- live_clusters: int32 [32], P(('group', 'inner')), may hold values from 4 to 12, as said below
- req_rows: int32 [32, 32, 16], P(('group', 'inner')), may hold values from 0 to 6143
- req_count: int32 [32, 32], P(('group', 'inner')), may hold values from 0 to 16, as said below
- req_target: int32 [32, 32, 16], P(('group', 'inner')), may hold values from 0 to 6143
- req_weight: float32 [32, 32, 16], P(('group', 'inner')), may hold values from 0.05 to 1
- hist_emb: bfloat16 [196608, 256], P(('group', 'inner')), may hold values from -6 to 6
- hist_grad: bfloat16 [196608, 256], P(('group', 'inner')), may hold values from -6 to 6
- layer_weight: bfloat16 [256, 256], replicated, may hold values from -0.375 to 0.375
- layer_bias: float32 [256], replicated, may hold values from -4 to 4
- cotangent: bfloat16 [196608, 256], P(('group', 'inner')), may hold values from -6 to 6
Outputs:
- input_grad: bfloat16 [196608, 256], P(('group', 'inner'))
- weight_grad: float32 [256, 256], replicated
- bias_grad: float32 [256], replicated
- owner_grad: bfloat16 [196608, 256], P(('group', 'inner'))
The draws below stay inside these ranges and needn't reach their ends.
Inputs may be any that keep to these rules, and one draw needn't show every extreme that they name: `live_clusters`: some device has all 12 cluster slots filled and some has only the fewest. `req_count`: in every draw each requesting device fills all 16 slots to some owner, and some owner receives 16 used slots from every device.
All inputs are finite; a program needn't handle non-finite values.
Results may differ from the reference program's by a relative error of at most 0.0063.
Values may be sent and summed in bfloat16 or wider, within the bound.
A program may use at most 128 MiB of HBM per device.

```python
import math
import jax
import jax.numpy as jnp
from jax import lax

F = 256
CLUSTER = 512
CLUS_DEV = 12
CAP = 16
NODES_DEV = 6144
PEERS = 32
NODES = 196608


def draw_live_clusters(key, part):
    fewest = max(1, CLUS_DEV // 3)
    values = jax.random.randint(jax.random.fold_in(key, 11), (PEERS,), fewest, CLUS_DEV + 1)
    order = jax.random.permutation(jax.random.fold_in(key, 12), PEERS)
    positions = jnp.arange(PEERS)
    values = jnp.where(positions == order[0], CLUS_DEV, values)
    values = jnp.where(positions == order[1], fewest, values)
    return values.astype(jnp.int32)


def draw_req_count(key, part):
    counts = jax.random.randint(jax.random.fold_in(key, 21), (PEERS, PEERS), 0, CAP + 1)
    shifts = jax.random.randint(jax.random.fold_in(key, 22), (PEERS,), 0, PEERS)
    full_owner = jax.random.randint(jax.random.fold_in(key, 23), (), 0, PEERS)
    sources = jnp.arange(PEERS)[:, None]
    owners = jnp.arange(PEERS)[None, :]
    counts = jnp.where(owners == (sources + shifts[:, None]) % PEERS, CAP, counts)
    counts = jnp.where(owners == full_owner, CAP, counts)
    return counts.astype(jnp.int32)


def place_ends(entries, stream_key, smallest, high):
    place = [jax.random.randint(jax.random.fold_in(stream_key, axis), (), 0, length) for axis, length in enumerate(entries.shape)]
    main_axis = entries.shape.index(max(entries.shape))
    neighbour = place[:main_axis] + [(place[main_axis] + 1) % entries.shape[main_axis]] + place[main_axis + 1:]
    return entries.at[tuple(place)].set(smallest).at[tuple(neighbour)].set(high)


def block_scale(own_key, dims, pieces, smallest, largest):
    def one(position, parts):
        steps = jax.random.uniform(jax.random.fold_in(jax.random.fold_in(own_key, 6), position), (parts,), jnp.float32, smallest / len(pieces), largest / len(pieces))
        return jnp.repeat(jnp.exp(steps), dims[position] // parts).reshape((-1,) + (1,) * (len(dims) - position - 1))

    factor_of = one(*pieces[0])
    for cut in pieces[1:]:
        factor_of = factor_of * one(*cut)
    return factor_of


def centred(key, shape, width, bound, split=(), held_as=jnp.bfloat16):
    loudness = block_scale(key, shape, split, -0.22, 0.18) if split else 1.0
    drawn = jax.random.normal(key, shape, jnp.float32) * width * loudness
    return jnp.minimum(jnp.maximum(drawn, -bound), bound).astype(held_as)


def setup_inputs(seed: int = 0) -> dict:
    splits = jax.random.split(jax.random.key(seed), 13)
    return {
        "node_feats": centred(splits[0], (NODES, F), 1.0, 6.0, ((0, 32),)),
        "adj_tiles": centred(splits[1], (NODES, CLUSTER), CLUSTER ** -0.5, 0.25, ((0, 32),)),
        "live_clusters": draw_live_clusters(jax.random.fold_in(splits[12], 71), 0),
        "req_rows": place_ends(jax.random.randint(splits[3], (PEERS, PEERS, CAP), 0, NODES_DEV), jax.random.fold_in(splits[3], 1), 0, NODES_DEV - 1).astype(jnp.int32),
        "req_count": draw_req_count(jax.random.fold_in(splits[12], 71), 0),
        "req_target": place_ends(jax.random.randint(splits[5], (PEERS, PEERS, CAP), 0, NODES_DEV), jax.random.fold_in(splits[5], 1), 0, NODES_DEV - 1).astype(jnp.int32),
        "req_weight": jnp.clip(jnp.exp(math.log(1.0) - 2.9957323 * jax.random.uniform(splits[6], (PEERS, PEERS, CAP), jnp.float32) ** block_scale(splits[6], (PEERS, PEERS, CAP), ((0, 32),), -0.2, 0.2)), 0.05, 1.0),
        "hist_emb": centred(splits[7], (NODES, F), 1.0, 6.0, ((0, 32),)),
        "hist_grad": centred(splits[8], (NODES, F), 1.0, 6.0, ((0, 32),)),
        "layer_weight": centred(splits[9], (F, F), F ** -0.5, 0.375),
        "layer_bias": centred(splits[10], (F,), 1.0, 4.0, (), jnp.float32),
        "cotangent": centred(splits[11], (NODES, F), 1.0, 6.0, ((0, 32),)),
    }


def gelu_slope(values):
    root_coef = math.sqrt(2.0 / math.pi)
    cube_coef = 0.044715
    tangent = jnp.tanh(root_coef * (values + cube_coef * values * values * values))
    return 0.5 * (1.0 + tangent) + 0.5 * values * (1.0 - tangent * tangent) * root_coef * (1.0 + 3.0 * cube_coef * values * values)

def reference(node_feats, adj_tiles, live_clusters, req_rows, req_count, req_target, req_weight, hist_emb, hist_grad, layer_weight, layer_bias, cotangent):
    emb_table = hist_emb.reshape(PEERS, NODES_DEV, F)
    grad_table = hist_grad.reshape(PEERS, NODES_DEV, F)
    owner_ids = jnp.arange(PEERS).astype(jnp.int32)[None, :, None]
    pulled_emb = emb_table[owner_ids, req_rows]
    pulled_grad = grad_table[owner_ids, req_rows]
    slot_used = jnp.arange(CAP).astype(jnp.int32)[None, None, :] < req_count[:, :, None]
    slot_scale = jnp.where(slot_used, req_weight, jnp.float32(0.0)).astype(jnp.float32)
    weight_f = layer_weight.astype(jnp.float32)

    def one_device(items):
        feats_d, adj_d, live_d, emb_d, grad_d, scale_d, target_d, cot_d = items
        targets = target_d.reshape(-1)
        adj_c = adj_d.astype(jnp.float32).reshape(CLUS_DEV, CLUSTER, CLUSTER)
        local_sum = jnp.einsum('cij,cjf->cif', adj_c, feats_d.astype(jnp.float32).reshape(CLUS_DEV, CLUSTER, F)).reshape(NODES_DEV, F)
        weights_col = scale_d.reshape(-1, 1)
        comp_emb = jax.ops.segment_sum(weights_col * emb_d.reshape(-1, F).astype(jnp.float32), targets, num_segments=NODES_DEV)
        aggregate = (local_sum + comp_emb).astype(jnp.bfloat16)
        pre_act = jnp.dot(aggregate, layer_weight, preferred_element_type=jnp.float32) + layer_bias
        live_rows = (jnp.arange(NODES_DEV).astype(jnp.int32) // CLUSTER < live_d).astype(jnp.float32)[:, None]
        grad_pre = cot_d.astype(jnp.float32) * gelu_slope(pre_act) * live_rows
        grad_low = grad_pre.astype(jnp.bfloat16)
        weight_part = jnp.dot(aggregate.T, grad_low, preferred_element_type=jnp.float32)
        bias_part = lax.optimization_barrier(jnp.sum(grad_pre, axis=0))
        feat_grad = jnp.dot(grad_low, layer_weight.T, preferred_element_type=jnp.float32).astype(jnp.bfloat16)
        comp_grad = jax.ops.segment_sum(weights_col * grad_d.reshape(-1, F).astype(jnp.float32), targets, num_segments=NODES_DEV).astype(jnp.bfloat16)
        back_sum = jnp.einsum('cji,cjf->cif', adj_c, feat_grad.astype(jnp.float32).reshape(CLUS_DEV, CLUSTER, F)).reshape(NODES_DEV, F)
        back_sum = back_sum + jnp.dot(comp_grad, layer_weight.T, preferred_element_type=jnp.float32)
        input_grad = (back_sum * live_rows).astype(jnp.bfloat16)
        message = (scale_d[:, :, None] * feat_grad[target_d].astype(jnp.float32)).astype(jnp.bfloat16)
        return (input_grad, weight_part, bias_part, message)
    items = (node_feats.reshape(PEERS, NODES_DEV, F), adj_tiles.reshape(PEERS, NODES_DEV, CLUSTER), live_clusters, pulled_emb, pulled_grad, slot_scale, req_target, cotangent.reshape(PEERS, NODES_DEV, F))
    input_grad, weight_parts, bias_parts, message = lax.map(one_device, items)
    norm_factor = float(NODES) ** (-0.5)
    weight_grad = lax.optimization_barrier(jnp.sum(weight_parts, axis=0)) * norm_factor
    bias_grad = lax.optimization_barrier(jnp.sum(bias_parts, axis=0)) * norm_factor
    flat_rows = (owner_ids * NODES_DEV + req_rows).reshape(-1)
    owner_grad = jax.ops.segment_sum(message.reshape(-1, F).astype(jnp.float32), flat_rows, num_segments=NODES).astype(jnp.bfloat16)
    return (input_grad.reshape(NODES, F), weight_grad, bias_grad, owner_grad)
```

```python
import functools
import math

import jax
import jax.numpy as jnp
from jax import lax
from jax.experimental import pallas as pl
from jax.experimental.pallas import tpu as pltpu
from jax.sharding import PartitionSpec as P

MESH = pl.DeviceIdType.MESH
BF = jnp.bfloat16
F32 = jnp.float32
NN = (((1,), (0,)), ((), ()))
NT = (((1,), (1,)), ((), ()))
TN = (((0,), (0,)), ((), ()))


def mm(a, b, dims=NN):
    return lax.dot_general(a, b, dims, preferred_element_type=F32)


def exact(a, b, dims=NN):
    return lax.dot_general(
        a, b, dims, preferred_element_type=F32, precision=lax.Precision.HIGHEST
    )


def iota(shape, dim):
    return lax.broadcasted_iota(jnp.int32, shape, dim)


def gelu_slope(z):
    root = math.sqrt(2.0 / math.pi)
    cube = 0.044715
    sq = z * z
    t = jnp.tanh(root * z * (1.0 + cube * sq))
    return 0.5 * (1.0 + t) + (0.5 * root) * z * (1.0 - t * t) * (1.0 + 3.0 * cube * sq)


def column_of(table, slots):
    peers = table.shape[1]
    total = peers * slots
    pick = (iota((total, slots), 0) % slots == iota((total, slots), 1)).astype(F32)
    wide = exact(pick, table)
    keep = iota((total, peers), 0) // slots == iota((total, peers), 1)
    return jnp.sum(jnp.where(keep, wide, 0.0), axis=1, keepdims=True)


def row_of(table, slots):
    peers = table.shape[1]
    total = peers * slots
    pick = (iota((peers, total), 1) // slots == iota((peers, total), 0)).astype(F32)
    wide = exact(table, pick)
    keep = iota((slots, total), 1) % slots == iota((slots, total), 0)
    return jnp.sum(jnp.where(keep, wide, 0.0), axis=0, keepdims=True)


def main_kernel(
    members, peers, reducers,
    live_ref, rows_ref, count_ref, target_ref, weight_ref, w_ref, bias_ref,
    feats_hbm, adj_hbm, cot_hbm, emb_hbm, grad_hbm,
    wanted_out, arrived_out, wg_out, bg_out, ig_hbm,
    feats, adj, cot, emb, grad, local, fg, ig,
    rq_send, rq_recv, e_send, e_recv, g_send, g_recv, m_send,
    rs_send, rs_recv, acc, mes, wacc, bacc,
    load_sem, adj_sem, out_sem, send_sem, recv_sem,
):
    nodes_dev, width = feats.shape
    cluster = adj.shape[1]
    clusters = nodes_dev // cluster
    slots = rows_ref.shape[0]
    total = peers * slots
    me = lax.axis_index("group") * members + lax.axis_index("inner")
    part = width // reducers
    chunk = rs_send.shape[0] // reducers

    def at(p):
        return (p // members, p % members)

    def tile(ref, c):
        return ref.at[pl.ds(pl.multiple_of(c * cluster, cluster), cluster)]

    loads = [
        pltpu.make_async_copy(src, dst, load_sem.at[i])
        for i, (src, dst) in enumerate(
            ((feats_hbm, feats), (emb_hbm, emb), (grad_hbm, grad), (cot_hbm, cot))
        )
    ]

    def adj_load(c):
        return pltpu.make_async_copy(tile(adj_hbm, c), tile(adj, c), adj_sem.at[c])

    loads[0].start()
    for c in range(clusters):
        adj_load(c).start()
    loads[1].start()
    loads[2].start()
    loads[3].start()

    barrier = pltpu.get_barrier_semaphore()

    @pl.loop(1, peers)
    def _(i):
        pl.semaphore_signal(
            barrier, inc=1, device_id=at(lax.rem(me + i, peers)), device_id_type=MESH
        )

    rows = rows_ref[...].astype(F32)
    rows = jnp.concatenate([rows, jnp.zeros((128 - slots, peers), F32)], axis=0)
    eye = (iota((peers, peers), 0) == iota((peers, peers), 1)).astype(F32)
    by_owner = exact(eye, rows, NT)
    for p in range(peers):
        rq_send[p] = by_owner[p : p + 1, :]
    rq_recv[me] = rq_send[me]

    pl.semaphore_wait(barrier, peers - 1)

    def to_all(phase, src_of, dst_of):
        @pl.loop(1, peers)
        def _(i):
            p = lax.rem(me + i, peers)
            pltpu.make_async_remote_copy(
                src_ref=src_of(p),
                dst_ref=dst_of(me),
                send_sem=send_sem.at[phase],
                recv_sem=recv_sem.at[phase],
                device_id=at(p),
                device_id_type=MESH,
            ).start()

    def wait_bytes(ref, sem):
        pltpu.make_async_copy(ref, ref, sem).wait()

    def rows_at(ref, size):
        return lambda p: ref.at[pl.ds(pl.multiple_of(p * size, size), size)]

    to_all(0, lambda p: rq_send.at[p], lambda p: rq_recv.at[p])

    loads[0].wait()

    @pl.loop(0, clusters)
    def _(c):
        adj_load(c).wait()
        tile(local, c)[...] = mm(tile(adj, c)[...], tile(feats, c)[...])

    wait_bytes(rq_recv.at[pl.ds(0, peers - 1)], recv_sem.at[0])
    wanted = jnp.concatenate([rq_recv[p] for p in range(peers)], axis=0)
    wanted_out[...] = wanted
    pick = (iota((total, peers), 0) // slots == iota((total, peers), 1)).astype(F32)
    wide = exact(pick, wanted)
    keep = iota((total, 128), 0) % slots == iota((total, 128), 1)
    wanted_col = jnp.sum(jnp.where(keep, wide, 0.0), axis=1, keepdims=True).astype(jnp.int32)
    lane = iota((total, cluster), 1)

    def gather(table, out):
        acc[...] = jnp.zeros_like(acc)

        @pl.loop(0, clusters)
        def _(c):
            one = jnp.where(wanted_col - c * cluster == lane, 1.0, 0.0).astype(BF)
            acc[...] += mm(one, tile(table, c)[...])

        out[...] = acc[...].astype(BF)

    own = pl.ds(pl.multiple_of(me * slots, slots), slots)
    loads[1].wait()
    gather(emb, e_send)
    e_recv[own, :] = e_send[own, :]
    to_all(1, rows_at(e_send, slots), rows_at(e_recv, slots))
    loads[2].wait()
    gather(grad, g_send)
    g_recv[own, :] = g_send[own, :]
    to_all(2, rows_at(g_send, slots), rows_at(g_recv, slots))

    used = iota((slots, peers), 0) < count_ref[...]
    scale_col = column_of(jnp.where(used, weight_ref[...], 0.0), slots)
    targets = target_ref[...].astype(F32)
    target_col = column_of(targets, slots).astype(jnp.int32)
    target_row = row_of(targets, slots).astype(jnp.int32)
    node = iota((cluster, total), 0)
    weights = w_ref[...]
    bias = bias_ref[...]
    mes[...] = jnp.zeros_like(mes)
    wacc[...] = jnp.zeros_like(wacc)
    bacc[...] = jnp.zeros_like(bacc)
    loads[3].wait()

    wait_bytes(e_recv.at[pl.ds(0, (peers - 1) * slots)], recv_sem.at[1])
    e_recv[...] = (scale_col * e_recv[...].astype(F32)).astype(BF)

    def live_of(c):
        return jnp.where(c < live_ref[0], 1.0, 0.0).astype(F32)

    @pl.loop(0, clusters)
    def _(c):
        spread = jnp.where(target_row - c * cluster == node, 1.0, 0.0).astype(BF)
        agg = (tile(local, c)[...] + mm(spread, e_recv[...])).astype(BF)
        pre = mm(agg, weights) + bias
        g = tile(cot, c)[...].astype(F32) * gelu_slope(pre) * live_of(c)
        low = g.astype(BF)
        bacc[...] += jnp.sum(g.reshape(cluster // 8, 8, width), axis=0)
        wacc[...] += mm(agg, low, TN)
        back = mm(low, weights, NT).astype(BF)
        tile(fg, c)[...] = back
        take = jnp.where(target_col - c * cluster == lane, 1.0, 0.0).astype(BF)
        mes[...] += mm(take, back)

    sums = bacc[...].astype(BF).astype(F32)
    for r in range(reducers):
        piece = wacc[r * part : (r + 1) * part, :]
        fill = chunk - part - 8
        both = [piece, sums] + ([jnp.zeros((fill, width), F32)] if fill else [])
        rs_send[r * chunk : (r + 1) * chunk, :] = jnp.concatenate(both, axis=0).astype(BF)
    slice_of = rows_at(rs_send, chunk)
    slot_of = rows_at(rs_recv, chunk)
    slot_of(me)[...] = slice_of(lax.rem(me, reducers))[...]
    to_all(3, lambda p: slice_of(lax.rem(p, reducers)), slot_of)
    m_send[...] = (scale_col * mes[...]).astype(BF)
    arrived_out[own, :] = m_send[own, :]
    to_all(4, rows_at(m_send, slots), rows_at(arrived_out, slots))

    wait_bytes(g_recv.at[pl.ds(0, (peers - 1) * slots)], recv_sem.at[2])
    scaled = (scale_col * g_recv[...].astype(F32)).astype(BF)
    e_recv[...] = mm(scaled, weights, NT).astype(BF)

    def out_copy(c):
        return pltpu.make_async_copy(tile(ig, c), tile(ig_hbm, c), out_sem)

    def backward(c):
        spread = jnp.where(target_row - c * cluster == node, 1.0, 0.0).astype(BF)
        back = mm(tile(adj, c)[...], tile(fg, c)[...], TN) + mm(spread, e_recv[...])
        tile(ig, c)[...] = (back * live_of(c)).astype(BF)
        out_copy(c).start()

    half = clusters // 2

    @pl.loop(0, half)
    def _(c):
        backward(c)

    wait_bytes(rs_recv.at[pl.ds(0, (peers - 1) * chunk)], recv_sem.at[3])
    norm = float(nodes_dev * peers) ** (-0.5)
    got = jnp.sum(rs_recv[...].astype(F32).reshape(peers, chunk, width), axis=0) * norm
    mine = lax.rem(me, reducers)
    part_of = rows_at(wg_out, part)
    part_of(mine)[...] = got[:part, :]
    bg_out[...] = jnp.sum(got[part : part + 8, :], axis=0, keepdims=True)

    def share():
        to_all(5, lambda p: part_of(me), part_of)

    if reducers == peers:
        share()
    else:
        pl.when(me < reducers)(share)

    @pl.loop(half, clusters)
    def _(c):
        backward(c)

    if reducers == peers:
        wait_bytes(wg_out.at[pl.ds(0, (peers - 1) * part)], recv_sem.at[5])
        wait_bytes(wg_out.at[pl.ds(0, (peers - 1) * part)], send_sem.at[5])
    else:
        @pl.when(me < reducers)
        def _():
            wait_bytes(wg_out.at[pl.ds(0, (reducers - 1) * part)], recv_sem.at[5])

            @pl.loop(1, peers)
            def _(i):
                wait_bytes(wg_out.at[pl.ds(0, part)], send_sem.at[5])

        @pl.when(me >= reducers)
        def _():
            wait_bytes(wg_out, recv_sem.at[5])

    wait_bytes(arrived_out.at[pl.ds(0, (peers - 1) * slots)], recv_sem.at[4])
    wait_bytes(rq_send.at[pl.ds(0, peers - 1)], send_sem.at[0])
    wait_bytes(e_send.at[pl.ds(0, (peers - 1) * slots)], send_sem.at[1])
    wait_bytes(g_send.at[pl.ds(0, (peers - 1) * slots)], send_sem.at[2])
    wait_bytes(rs_recv.at[pl.ds(0, (peers - 1) * chunk)], send_sem.at[3])
    wait_bytes(m_send.at[pl.ds(0, (peers - 1) * slots)], send_sem.at[4])
    wait_bytes(ig, out_sem)


def owner_kernel(slots, wanted_ref, arrived_ref, ig_ref, out_ref, ig_out, row_scr):
    step = pl.program_id(0)
    peers = wanted_ref.shape[0]
    total = peers * slots

    @pl.when(step == 0)
    def _():
        pick = (iota((peers, total), 1) // slots == iota((peers, total), 0)).astype(F32)
        wide = exact(wanted_ref[...], pick, TN)
        keep = iota((128, total), 1) % slots == iota((128, total), 0)
        row = jnp.sum(jnp.where(keep, wide, 0.0), axis=0, keepdims=True)
        row_scr[...] = row.astype(jnp.int32)

    size = out_ref.shape[0]
    spread = jnp.where(row_scr[...] - step * size == iota((size, total), 0), 1.0, 0.0)
    out_ref[...] = mm(spread.astype(BF), arrived_ref[...]).astype(BF)
    ig_out[...] = ig_ref[...]


def on_device(
    node_feats, adj_tiles, live_clusters, req_rows, req_count, req_target, req_weight,
    hist_emb, hist_grad, layer_weight, layer_bias, cotangent,
):
    nodes_dev, width = node_feats.shape
    cluster = adj_tiles.shape[1]
    clusters = nodes_dev // cluster
    peers, slots = req_rows.shape[1:]
    members = lax.axis_size("inner")
    total = peers * slots
    reducers = min(peers, 32)
    part = width // reducers
    chunk = -(-(part + 8) // 16) * 16
    flip = lambda a: jnp.transpose(a[0])
    vmem = pl.BlockSpec(memory_space=pltpu.VMEM)
    hbm = pl.BlockSpec(memory_space=pl.ANY)
    sds = jax.ShapeDtypeStruct
    full = (nodes_dev, width)
    wanted, arrived, wg, bg, ig = pl.pallas_call(
        functools.partial(main_kernel, members, peers, reducers),
        out_shape=(
            sds((peers, 128), F32),
            sds((total, width), BF),
            sds((width, width), F32),
            sds((1, width), F32),
            sds(full, BF),
        ),
        in_specs=[pl.BlockSpec(memory_space=pltpu.SMEM)] + [vmem] * 6 + [hbm] * 5,
        out_specs=(vmem, vmem, vmem, vmem, hbm),
        scratch_shapes=[
            pltpu.VMEM(full, BF),
            pltpu.VMEM((nodes_dev, cluster), BF),
            pltpu.VMEM(full, BF),
            pltpu.VMEM(full, BF),
            pltpu.VMEM(full, BF),
            pltpu.VMEM(full, F32),
            pltpu.VMEM(full, BF),
            pltpu.VMEM(full, BF),
            pltpu.VMEM((peers, 1, 128), F32),
            pltpu.VMEM((peers, 1, 128), F32),
            pltpu.VMEM((total, width), BF),
            pltpu.VMEM((total, width), BF),
            pltpu.VMEM((total, width), BF),
            pltpu.VMEM((total, width), BF),
            pltpu.VMEM((total, width), BF),
            pltpu.VMEM((reducers * chunk, width), BF),
            pltpu.VMEM((peers * chunk, width), BF),
            pltpu.VMEM((total, width), F32),
            pltpu.VMEM((total, width), F32),
            pltpu.VMEM((width, width), F32),
            pltpu.VMEM((8, width), F32),
            pltpu.SemaphoreType.DMA((4,)),
            pltpu.SemaphoreType.DMA((clusters,)),
            pltpu.SemaphoreType.DMA,
            pltpu.SemaphoreType.DMA((6,)),
            pltpu.SemaphoreType.DMA((6,)),
        ],
        compiler_params=pltpu.CompilerParams(
            collective_id=0, has_side_effects=True, vmem_limit_bytes=58 * 1024 * 1024
        ),
    )(
        live_clusters, flip(req_rows), req_count, flip(req_target), flip(req_weight),
        layer_weight, layer_bias[None, :],
        node_feats, adj_tiles, cotangent, hist_emb, hist_grad,
    )
    whole = lambda a: pl.BlockSpec(a.shape, lambda i: (0, 0))
    tiles = pl.BlockSpec((cluster, width), lambda i: (i, 0))
    owner_grad, input_grad = pl.pallas_call(
        functools.partial(owner_kernel, slots),
        grid=(clusters,),
        out_shape=(sds(full, BF), sds(full, BF)),
        in_specs=[whole(wanted), whole(arrived), tiles],
        out_specs=(tiles, tiles),
        scratch_shapes=[pltpu.VMEM((1, total), jnp.int32)],
        compiler_params=pltpu.CompilerParams(vmem_limit_bytes=32 * 1024 * 1024),
    )(wanted, arrived, ig)
    return input_grad, wg, bg[0], owner_grad


def solution(mesh):
    both = ("group", "inner")
    return jax.shard_map(
        on_device,
        mesh=mesh,
        in_specs=(
            P(both, None), P(both, None), P(both), P(both, None, None), P(both, None),
            P(both, None, None), P(both, None, None), P(both, None), P(both, None),
            P(), P(), P(both, None),
        ),
        out_specs=(P(both, None), P(), P(), P(both, None)),
        check_vma=False,
    )
```

```python
import functools
import math

import jax
import jax.numpy as jnp
from jax import lax
from jax.experimental import pallas as pl
from jax.experimental.pallas import tpu as pltpu
from jax.sharding import PartitionSpec as P

MESH = pl.DeviceIdType.MESH
BF = jnp.bfloat16
F32 = jnp.float32
NN = (((1,), (0,)), ((), ()))
NT = (((1,), (1,)), ((), ()))
TN = (((0,), (0,)), ((), ()))


def mm(a, b, dims=NN):
    return lax.dot_general(a, b, dims, preferred_element_type=F32)


def exact(a, b, dims=NN):
    return lax.dot_general(
        a, b, dims, preferred_element_type=F32, precision=lax.Precision.HIGHEST
    )


def iota(shape, dim):
    return lax.broadcasted_iota(jnp.int32, shape, dim)


def gelu_slope(z):
    root = math.sqrt(2.0 / math.pi)
    cube = 0.044715
    sq = z * z
    t = jnp.tanh(root * z * (1.0 + cube * sq))
    return 0.5 * (1.0 + t) + (0.5 * root) * z * (1.0 - t * t) * (1.0 + 3.0 * cube * sq)


def column_of(table, slots):
    peers = table.shape[1]
    total = peers * slots
    pick = (iota((total, slots), 0) % slots == iota((total, slots), 1)).astype(F32)
    wide = exact(pick, table)
    keep = iota((total, peers), 0) // slots == iota((total, peers), 1)
    return jnp.sum(jnp.where(keep, wide, 0.0), axis=1, keepdims=True)


def row_of(table, slots):
    peers = table.shape[1]
    total = peers * slots
    pick = (iota((peers, total), 1) // slots == iota((peers, total), 0)).astype(F32)
    wide = exact(table, pick)
    keep = iota((slots, total), 1) % slots == iota((slots, total), 0)
    return jnp.sum(jnp.where(keep, wide, 0.0), axis=0, keepdims=True)


def main_kernel(
    members, peers, reducers,
    live_ref, rows_ref, count_ref, target_ref, weight_ref, w_ref, bias_ref,
    feats_hbm, adj_hbm, cot_hbm, emb_hbm, grad_hbm,
    wanted_out, arrived_out, wg_out, bg_out, ig_hbm,
    feats, adj, cot, emb, grad, local, fg, ig,
    rq_send, rq_recv, e_send, e_recv, g_send, g_recv, m_send,
    rs_send, rs_recv, ws, bs, acc, mes, wacc, bacc,
    load_sem, adj_sem, out_sem, send_sem, recv_sem,
):
    nodes_dev, width = feats.shape
    cluster = adj.shape[1]
    clusters = nodes_dev // cluster
    slots = rows_ref.shape[0]
    total = peers * slots
    me = lax.axis_index("group") * members + lax.axis_index("inner")
    part = width // reducers
    chunk = 2 * part
    lanes = width // 2

    def at(p):
        return (p // members, p % members)

    def tile(ref, c):
        return ref.at[pl.ds(pl.multiple_of(c * cluster, cluster), cluster)]

    loads = [
        pltpu.make_async_copy(src, dst, load_sem.at[i])
        for i, (src, dst) in enumerate(
            ((feats_hbm, feats), (emb_hbm, emb), (grad_hbm, grad), (cot_hbm, cot))
        )
    ]

    def adj_load(c):
        return pltpu.make_async_copy(tile(adj_hbm, c), tile(adj, c), adj_sem.at[c])

    loads[0].start()
    for c in range(clusters):
        adj_load(c).start()
    loads[1].start()
    loads[2].start()
    loads[3].start()

    barrier = pltpu.get_barrier_semaphore()

    @pl.loop(1, peers)
    def _(i):
        pl.semaphore_signal(
            barrier, inc=1, device_id=at(lax.rem(me + i, peers)), device_id_type=MESH
        )

    rows = rows_ref[...].astype(F32)
    rows = jnp.concatenate([rows, jnp.zeros((128 - slots, peers), F32)], axis=0)
    eye = (iota((peers, peers), 0) == iota((peers, peers), 1)).astype(F32)
    by_owner = exact(eye, rows, NT)
    for p in range(peers):
        rq_send[p] = by_owner[p : p + 1, :]
    rq_recv[me] = rq_send[me]

    pl.semaphore_wait(barrier, peers - 1)

    def to_all(phase, src_of, dst_of):
        @pl.loop(1, peers)
        def _(i):
            p = lax.rem(me + i, peers)
            pltpu.make_async_remote_copy(
                src_ref=src_of(p),
                dst_ref=dst_of(me),
                send_sem=send_sem.at[phase],
                recv_sem=recv_sem.at[phase],
                device_id=at(p),
                device_id_type=MESH,
            ).start()

    def wait_bytes(ref, sem):
        pltpu.make_async_copy(ref, ref, sem).wait()

    def rows_at(ref, size):
        return lambda p: ref.at[pl.ds(pl.multiple_of(p * size, size), size)]

    to_all(0, lambda p: rq_send.at[p], lambda p: rq_recv.at[p])

    loads[0].wait()

    @pl.loop(0, clusters)
    def _(c):
        adj_load(c).wait()
        tile(local, c)[...] = mm(tile(adj, c)[...], tile(feats, c)[...])

    wait_bytes(rq_recv.at[pl.ds(0, peers - 1)], recv_sem.at[0])
    wanted = jnp.concatenate([rq_recv[p] for p in range(peers)], axis=0)
    pick = (iota((total, peers), 0) // slots == iota((total, peers), 1)).astype(F32)
    wide = exact(pick, wanted)
    keep = iota((total, 128), 0) % slots == iota((total, 128), 1)
    wanted_col = jnp.sum(jnp.where(keep, wide, 0.0), axis=1, keepdims=True).astype(jnp.int32)
    flat = iota((peers, total), 1) // slots == iota((peers, total), 0)
    wide = exact(wanted, flat.astype(F32), TN)
    keep = iota((128, total), 1) % slots == iota((128, total), 0)
    wanted_out[...] = jnp.sum(jnp.where(keep, wide, 0.0), axis=0, keepdims=True).astype(jnp.int32)
    lane = iota((total, cluster), 1)

    def gather(table, out):
        acc[...] = jnp.zeros_like(acc)

        @pl.loop(0, clusters, unroll=4)
        def _(c):
            one = jnp.where(wanted_col - c * cluster == lane, 1.0, 0.0).astype(BF)
            acc[...] += mm(one, tile(table, c)[...])

        out[...] = acc[...].astype(BF)

    own = pl.ds(pl.multiple_of(me * slots, slots), slots)
    loads[1].wait()
    gather(emb, e_send)
    e_recv[own, :] = e_send[own, :]
    to_all(1, rows_at(e_send, slots), rows_at(e_recv, slots))
    loads[2].wait()
    gather(grad, g_send)
    g_recv[own, :] = g_send[own, :]
    to_all(2, rows_at(g_send, slots), rows_at(g_recv, slots))

    used = iota((slots, peers), 0) < count_ref[...]
    scale_col = column_of(jnp.where(used, weight_ref[...], 0.0), slots)
    targets = target_ref[...].astype(F32)
    target_col = column_of(targets, slots).astype(jnp.int32)
    target_row = row_of(targets, slots).astype(jnp.int32)
    node = iota((cluster, total), 0)
    weights = w_ref[...]
    bias = bias_ref[...]
    mes[...] = jnp.zeros_like(mes)
    wacc[...] = jnp.zeros_like(wacc)
    bacc[...] = jnp.zeros_like(bacc)
    loads[3].wait()

    wait_bytes(e_recv.at[pl.ds(0, (peers - 1) * slots)], recv_sem.at[1])
    e_recv[...] = (scale_col * e_recv[...].astype(F32)).astype(BF)

    def live_of(c):
        return jnp.where(c < live_ref[0], 1.0, 0.0).astype(F32)

    @pl.loop(0, clusters, unroll=3)
    def _(c):
        spread = jnp.where(target_row - c * cluster == node, 1.0, 0.0).astype(BF)
        agg = (tile(local, c)[...] + mm(spread, e_recv[...])).astype(BF)
        pre = mm(agg, weights) + bias
        g = tile(cot, c)[...].astype(F32) * gelu_slope(pre) * live_of(c)
        low = g.astype(BF)
        bacc[...] += jnp.sum(g.reshape(cluster // 8, 8, width), axis=0)
        tile(feats, c)[...] = agg
        tile(cot, c)[...] = low
        back = mm(low, weights, NT).astype(BF)
        tile(fg, c)[...] = back
        take = jnp.where(target_col - c * cluster == lane, 1.0, 0.0).astype(BF)
        mes[...] += mm(take, back)

    m_send[...] = (scale_col * mes[...]).astype(BF)
    arrived_out[own, :] = m_send[own, :]
    to_all(4, rows_at(m_send, slots), rows_at(arrived_out, slots))

    @pl.loop(0, clusters)
    def _(c):
        wacc[...] += mm(tile(feats, c)[...], tile(cot, c)[...], TN)

    pairs = []
    for r in range(reducers):
        piece = wacc[r * part : (r + 1) * part, :]
        pairs += [piece[:, :lanes], piece[:, lanes:]]
    rs_send[...] = jnp.concatenate(pairs, axis=0).astype(BF)
    slice_of = rows_at(rs_send, chunk)
    slot_of = rows_at(rs_recv, chunk)
    slot_of(me)[...] = slice_of(lax.rem(me, reducers))[...]
    to_all(3, lambda p: slice_of(lax.rem(p, reducers)), slot_of)
    bs[me] = jnp.sum(bacc[...], axis=0, keepdims=True)
    to_all(6, lambda p: bs.at[me], lambda p: bs.at[p])

    wait_bytes(g_recv.at[pl.ds(0, (peers - 1) * slots)], recv_sem.at[2])
    scaled = (scale_col * g_recv[...].astype(F32)).astype(BF)
    e_recv[...] = mm(scaled, weights, NT).astype(BF)

    def out_copy(c):
        return pltpu.make_async_copy(tile(ig, c), tile(ig_hbm, c), out_sem)

    def backward(c):
        spread = jnp.where(target_row - c * cluster == node, 1.0, 0.0).astype(BF)
        back = mm(tile(adj, c)[...], tile(fg, c)[...], TN) + mm(spread, e_recv[...])
        tile(ig, c)[...] = (back * live_of(c)).astype(BF)
        out_copy(c).start()

    half = clusters // 2

    @pl.loop(0, half)
    def _(c):
        backward(c)

    wait_bytes(rs_recv.at[pl.ds(0, (peers - 1) * chunk)], recv_sem.at[3])
    norm = float(nodes_dev * peers) ** (-0.5)
    got = jnp.sum(rs_recv[...].astype(F32).reshape(peers, chunk, lanes), axis=0) * norm
    part_of = rows_at(ws, chunk)
    part_of(lax.rem(me, reducers))[...] = got.astype(BF)

    def share():
        to_all(5, lambda p: part_of(me), part_of)

    if reducers == peers:
        share()
    else:
        pl.when(me < reducers)(share)

    @pl.loop(half, clusters)
    def _(c):
        backward(c)

    if reducers == peers:
        wait_bytes(ws.at[pl.ds(0, (peers - 1) * chunk)], recv_sem.at[5])
        wait_bytes(ws.at[pl.ds(0, (peers - 1) * chunk)], send_sem.at[5])
    else:
        @pl.when(me < reducers)
        def _():
            wait_bytes(ws.at[pl.ds(0, (reducers - 1) * chunk)], recv_sem.at[5])

            @pl.loop(1, peers)
            def _(i):
                wait_bytes(ws.at[pl.ds(0, chunk)], send_sem.at[5])

        @pl.when(me >= reducers)
        def _():
            wait_bytes(ws, recv_sem.at[5])

    halves = ws[...].astype(F32).reshape(reducers, 2, part, lanes)
    joined = jnp.concatenate([halves[:, 0], halves[:, 1]], axis=-1)
    wg_out[...] = joined.reshape(width, width)
    wait_bytes(bs.at[pl.ds(0, peers - 1)], recv_sem.at[6])
    wait_bytes(bs.at[pl.ds(0, peers - 1)], send_sem.at[6])
    bg_out[...] = jnp.sum(bs[...], axis=0) * norm
    wait_bytes(arrived_out.at[pl.ds(0, (peers - 1) * slots)], recv_sem.at[4])
    wait_bytes(rq_send.at[pl.ds(0, peers - 1)], send_sem.at[0])
    wait_bytes(e_send.at[pl.ds(0, (peers - 1) * slots)], send_sem.at[1])
    wait_bytes(g_send.at[pl.ds(0, (peers - 1) * slots)], send_sem.at[2])
    wait_bytes(rs_recv.at[pl.ds(0, (peers - 1) * chunk)], send_sem.at[3])
    wait_bytes(m_send.at[pl.ds(0, (peers - 1) * slots)], send_sem.at[4])
    wait_bytes(ig, out_sem)


def owner_kernel(
    wanted_ref, arrived_ref, wg_ref, bg_ref, ig_ref, out_ref, ig_out, wg_out, bg_out
):
    step = pl.program_id(0)

    @pl.when(step == 0)
    def _():
        wg_out[...] = wg_ref[...]
        bg_out[...] = bg_ref[0]

    size = out_ref.shape[0]
    total = arrived_ref.shape[0]
    spread = jnp.where(wanted_ref[...] - step * size == iota((size, total), 0), 1.0, 0.0)
    out_ref[...] = mm(spread.astype(BF), arrived_ref[...]).astype(BF)
    ig_out[...] = ig_ref[...]


def on_device(
    node_feats, adj_tiles, live_clusters, req_rows, req_count, req_target, req_weight,
    hist_emb, hist_grad, layer_weight, layer_bias, cotangent,
):
    nodes_dev, width = node_feats.shape
    cluster = adj_tiles.shape[1]
    clusters = nodes_dev // cluster
    peers, slots = req_rows.shape[1:]
    members = lax.axis_size("inner")
    total = peers * slots
    reducers = min(peers, 32)
    part = width // reducers
    chunk, lanes = 2 * part, width // 2
    flip = lambda a: jnp.transpose(a[0])
    vmem = pl.BlockSpec(memory_space=pltpu.VMEM)
    hbm = pl.BlockSpec(memory_space=pl.ANY)
    sds = jax.ShapeDtypeStruct
    full = (nodes_dev, width)
    wanted, arrived, wg, bg, ig = pl.pallas_call(
        functools.partial(main_kernel, members, peers, reducers),
        out_shape=(
            sds((1, total), jnp.int32),
            sds((total, width), BF),
            sds((width, width), F32),
            sds((1, width), F32),
            sds(full, BF),
        ),
        in_specs=[pl.BlockSpec(memory_space=pltpu.SMEM)] + [vmem] * 6 + [hbm] * 5,
        out_specs=(vmem, vmem, vmem, vmem, hbm),
        scratch_shapes=[
            pltpu.VMEM(full, BF),
            pltpu.VMEM((nodes_dev, cluster), BF),
            pltpu.VMEM(full, BF),
            pltpu.VMEM(full, BF),
            pltpu.VMEM(full, BF),
            pltpu.VMEM(full, F32),
            pltpu.VMEM(full, BF),
            pltpu.VMEM(full, BF),
            pltpu.VMEM((peers, 1, 128), F32),
            pltpu.VMEM((peers, 1, 128), F32),
            pltpu.VMEM((total, width), BF),
            pltpu.VMEM((total, width), BF),
            pltpu.VMEM((total, width), BF),
            pltpu.VMEM((total, width), BF),
            pltpu.VMEM((total, width), BF),
            pltpu.VMEM((reducers * chunk, lanes), BF),
            pltpu.VMEM((peers * chunk, lanes), BF),
            pltpu.VMEM((reducers * chunk, lanes), BF),
            pltpu.VMEM((peers, 1, width), F32),
            pltpu.VMEM((total, width), F32),
            pltpu.VMEM((total, width), F32),
            pltpu.VMEM((width, width), F32),
            pltpu.VMEM((8, width), F32),
            pltpu.SemaphoreType.DMA((4,)),
            pltpu.SemaphoreType.DMA((clusters,)),
            pltpu.SemaphoreType.DMA,
            pltpu.SemaphoreType.DMA((7,)),
            pltpu.SemaphoreType.DMA((7,)),
        ],
        compiler_params=pltpu.CompilerParams(
            collective_id=0, has_side_effects=True, vmem_limit_bytes=58 * 1024 * 1024
        ),
    )(
        live_clusters, flip(req_rows), req_count, flip(req_target), flip(req_weight),
        layer_weight, layer_bias[None, :],
        node_feats, adj_tiles, cotangent, hist_emb, hist_grad,
    )
    whole = lambda a: pl.BlockSpec(a.shape, lambda i: (0,) * len(a.shape))
    per_step = 2 if clusters % 2 == 0 else 1
    tiles = pl.BlockSpec((per_step * cluster, width), lambda i: (i, 0))
    bias_out = sds((width,), F32)
    owner_grad, input_grad, weight_grad, bias_grad = pl.pallas_call(
        owner_kernel,
        grid=(clusters // per_step,),
        out_shape=(sds(full, BF), sds(full, BF), sds(wg.shape, F32), bias_out),
        in_specs=[whole(wanted), whole(arrived), whole(wg), whole(bg), tiles],
        out_specs=(tiles, tiles, whole(wg), whole(bias_out)),
        compiler_params=pltpu.CompilerParams(vmem_limit_bytes=60 * 1024 * 1024),
    )(wanted, arrived, wg, bg, ig)
    return input_grad, weight_grad, bias_grad, owner_grad


def solution(mesh):
    both = ("group", "inner")
    return jax.shard_map(
        on_device,
        mesh=mesh,
        in_specs=(
            P(both, None), P(both, None), P(both), P(both, None, None), P(both, None),
            P(both, None, None), P(both, None, None), P(both, None), P(both, None),
            P(), P(), P(both, None),
        ),
        out_specs=(P(both, None), P(), P(), P(both, None)),
        check_vma=False,
    )
```

```python
import functools
import math

import jax
import jax.numpy as jnp
from jax import lax
from jax.experimental import pallas as pl
from jax.experimental.pallas import tpu as pltpu
from jax.sharding import PartitionSpec as P

MESH = pl.DeviceIdType.MESH
BF = jnp.bfloat16
F32 = jnp.float32
NN = (((1,), (0,)), ((), ()))
NT = (((1,), (1,)), ((), ()))
TN = (((0,), (0,)), ((), ()))


def mm(a, b, dims=NN):
    return lax.dot_general(a, b, dims, preferred_element_type=F32)


def exact(a, b, dims=NN):
    return lax.dot_general(
        a, b, dims, preferred_element_type=F32, precision=lax.Precision.HIGHEST
    )


def iota(shape, dim):
    return lax.broadcasted_iota(jnp.int32, shape, dim)


def gelu_slope(z):
    root = math.sqrt(2.0 / math.pi)
    cube = 0.044715
    sq = z * z
    t = jnp.tanh(root * z * (1.0 + cube * sq))
    return 0.5 * (1.0 + t) + (0.5 * root) * z * (1.0 - t * t) * (1.0 + 3.0 * cube * sq)


def column_of(table, slots):
    peers = table.shape[1]
    total = peers * slots
    pick = (iota((total, slots), 0) % slots == iota((total, slots), 1)).astype(F32)
    wide = exact(pick, table)
    keep = iota((total, peers), 0) // slots == iota((total, peers), 1)
    return jnp.sum(jnp.where(keep, wide, 0.0), axis=1, keepdims=True)


def row_of(table, slots):
    peers = table.shape[1]
    total = peers * slots
    pick = (iota((peers, total), 1) // slots == iota((peers, total), 0)).astype(F32)
    wide = exact(table, pick)
    keep = iota((slots, total), 1) % slots == iota((slots, total), 0)
    return jnp.sum(jnp.where(keep, wide, 0.0), axis=0, keepdims=True)


def main_kernel(
    members, peers, reducers,
    live_ref, rows_ref, count_ref, target_ref, weight_ref, w_ref, bias_ref,
    feats_hbm, adj_hbm, cot_hbm, emb_hbm, grad_hbm,
    wg_out, bg_out, ig_hbm, og_hbm,
    feats, adj, cot, emb, grad, local, fg, ig,
    rq_send, rq_recv, e_send, e_recv, g_send, g_recv, m_send,
    rs_send, rs_recv, ws, bs, arrived_out, acc, mes, wacc, bacc,
    load_sem, adj_sem, out_sem, og_sem, send_sem, recv_sem,
):
    nodes_dev, width = feats.shape
    cluster = adj.shape[1]
    clusters = nodes_dev // cluster
    slots = rows_ref.shape[0]
    total = peers * slots
    me = lax.axis_index("group") * members + lax.axis_index("inner")
    part = width // reducers
    chunk = 2 * part
    lanes = width // 2

    def at(p):
        return (p // members, p % members)

    def tile(ref, c):
        return ref.at[pl.ds(pl.multiple_of(c * cluster, cluster), cluster)]

    loads = [
        pltpu.make_async_copy(src, dst, load_sem.at[i])
        for i, (src, dst) in enumerate(
            ((feats_hbm, feats), (emb_hbm, emb), (grad_hbm, grad), (cot_hbm, cot))
        )
    ]

    def adj_load(c):
        return pltpu.make_async_copy(tile(adj_hbm, c), tile(adj, c), adj_sem.at[c])

    loads[0].start()
    for c in range(clusters):
        adj_load(c).start()
    loads[1].start()
    loads[2].start()
    loads[3].start()

    barrier = pltpu.get_barrier_semaphore()

    @pl.loop(1, peers)
    def _(i):
        pl.semaphore_signal(
            barrier, inc=1, device_id=at(lax.rem(me + i, peers)), device_id_type=MESH
        )

    rows = rows_ref[...].astype(F32)
    rows = jnp.concatenate([rows, jnp.zeros((128 - slots, peers), F32)], axis=0)
    eye = (iota((peers, peers), 0) == iota((peers, peers), 1)).astype(F32)
    by_owner = exact(eye, rows, NT)
    for p in range(peers):
        rq_send[p] = by_owner[p : p + 1, :]
    rq_recv[me] = rq_send[me]

    pl.semaphore_wait(barrier, peers - 1)

    def to_all(phase, src_of, dst_of):
        @pl.loop(1, peers)
        def _(i):
            p = lax.rem(me + i, peers)
            pltpu.make_async_remote_copy(
                src_ref=src_of(p),
                dst_ref=dst_of(me),
                send_sem=send_sem.at[phase],
                recv_sem=recv_sem.at[phase],
                device_id=at(p),
                device_id_type=MESH,
            ).start()

    def wait_bytes(ref, sem):
        pltpu.make_async_copy(ref, ref, sem).wait()

    def rows_at(ref, size):
        return lambda p: ref.at[pl.ds(pl.multiple_of(p * size, size), size)]

    to_all(0, lambda p: rq_send.at[p], lambda p: rq_recv.at[p])

    loads[0].wait()

    @pl.loop(0, clusters)
    def _(c):
        adj_load(c).wait()
        tile(local, c)[...] = mm(tile(adj, c)[...], tile(feats, c)[...])

    wait_bytes(rq_recv.at[pl.ds(0, peers - 1)], recv_sem.at[0])
    wanted = jnp.concatenate([rq_recv[p] for p in range(peers)], axis=0)
    pick = (iota((total, peers), 0) // slots == iota((total, peers), 1)).astype(F32)
    wide = exact(pick, wanted)
    keep = iota((total, 128), 0) % slots == iota((total, 128), 1)
    wanted_col = jnp.sum(jnp.where(keep, wide, 0.0), axis=1, keepdims=True).astype(jnp.int32)
    flat = iota((peers, total), 1) // slots == iota((peers, total), 0)
    wide = exact(wanted, flat.astype(F32), TN)
    keep = iota((128, total), 1) % slots == iota((128, total), 0)
    wanted_row = jnp.sum(jnp.where(keep, wide, 0.0), axis=0, keepdims=True).astype(jnp.int32)
    lane = iota((total, cluster), 1)

    def gather(table, out):
        acc[...] = jnp.zeros_like(acc)

        @pl.loop(0, clusters, unroll=4)
        def _(c):
            one = jnp.where(wanted_col - c * cluster == lane, 1.0, 0.0).astype(BF)
            acc[...] += mm(one, tile(table, c)[...])

        out[...] = acc[...].astype(BF)

    own = pl.ds(pl.multiple_of(me * slots, slots), slots)
    loads[1].wait()
    gather(emb, e_send)
    e_recv[own, :] = e_send[own, :]
    to_all(1, rows_at(e_send, slots), rows_at(e_recv, slots))
    loads[2].wait()
    gather(grad, g_send)
    g_recv[own, :] = g_send[own, :]
    to_all(2, rows_at(g_send, slots), rows_at(g_recv, slots))

    used = iota((slots, peers), 0) < count_ref[...]
    scale_col = column_of(jnp.where(used, weight_ref[...], 0.0), slots)
    targets = target_ref[...].astype(F32)
    target_col = column_of(targets, slots).astype(jnp.int32)
    target_row = row_of(targets, slots).astype(jnp.int32)
    node = iota((cluster, total), 0)
    weights = w_ref[...]
    bias = bias_ref[...]
    mes[...] = jnp.zeros_like(mes)
    wacc[...] = jnp.zeros_like(wacc)
    bacc[...] = jnp.zeros_like(bacc)
    loads[3].wait()

    wait_bytes(e_recv.at[pl.ds(0, (peers - 1) * slots)], recv_sem.at[1])
    e_recv[...] = (scale_col * e_recv[...].astype(F32)).astype(BF)

    def live_of(c):
        return jnp.where(c < live_ref[0], 1.0, 0.0).astype(F32)

    @pl.loop(0, clusters, unroll=3)
    def _(c):
        spread = jnp.where(target_row - c * cluster == node, 1.0, 0.0).astype(BF)
        agg = (tile(local, c)[...] + mm(spread, e_recv[...])).astype(BF)
        pre = mm(agg, weights) + bias
        g = tile(cot, c)[...].astype(F32) * gelu_slope(pre) * live_of(c)
        low = g.astype(BF)
        bacc[...] += jnp.sum(g.reshape(cluster // 8, 8, width), axis=0)
        tile(feats, c)[...] = agg
        tile(cot, c)[...] = low
        back = mm(low, weights, NT).astype(BF)
        tile(fg, c)[...] = back
        take = jnp.where(target_col - c * cluster == lane, 1.0, 0.0).astype(BF)
        mes[...] += mm(take, back)

    m_send[...] = (scale_col * mes[...]).astype(BF)
    arrived_out[own, :] = m_send[own, :]
    to_all(4, rows_at(m_send, slots), rows_at(arrived_out, slots))

    @pl.loop(0, clusters)
    def _(c):
        wacc[...] += mm(tile(feats, c)[...], tile(cot, c)[...], TN)

    pairs = []
    for r in range(reducers):
        piece = wacc[r * part : (r + 1) * part, :]
        pairs += [piece[:, :lanes], piece[:, lanes:]]
    rs_send[...] = jnp.concatenate(pairs, axis=0).astype(BF)
    slice_of = rows_at(rs_send, chunk)
    slot_of = rows_at(rs_recv, chunk)
    slot_of(me)[...] = slice_of(lax.rem(me, reducers))[...]
    to_all(3, lambda p: slice_of(lax.rem(p, reducers)), slot_of)
    bs[me] = jnp.sum(bacc[...], axis=0, keepdims=True)
    to_all(6, lambda p: bs.at[me], lambda p: bs.at[p])

    wait_bytes(g_recv.at[pl.ds(0, (peers - 1) * slots)], recv_sem.at[2])
    scaled = (scale_col * g_recv[...].astype(F32)).astype(BF)
    e_recv[...] = mm(scaled, weights, NT).astype(BF)

    def out_copy(c):
        return pltpu.make_async_copy(tile(ig, c), tile(ig_hbm, c), out_sem)

    def backward(c):
        spread = jnp.where(target_row - c * cluster == node, 1.0, 0.0).astype(BF)
        back = mm(tile(adj, c)[...], tile(fg, c)[...], TN) + mm(spread, e_recv[...])
        tile(ig, c)[...] = (back * live_of(c)).astype(BF)
        out_copy(c).start()

    half = clusters // 2

    @pl.loop(0, half)
    def _(c):
        backward(c)

    wait_bytes(rs_recv.at[pl.ds(0, (peers - 1) * chunk)], recv_sem.at[3])
    norm = float(nodes_dev * peers) ** (-0.5)
    got = jnp.sum(rs_recv[...].astype(F32).reshape(peers, chunk, lanes), axis=0) * norm
    part_of = rows_at(ws, chunk)
    part_of(lax.rem(me, reducers))[...] = got.astype(BF)

    def share():
        to_all(5, lambda p: part_of(me), part_of)

    if reducers == peers:
        share()
    else:
        pl.when(me < reducers)(share)

    @pl.loop(half, clusters)
    def _(c):
        backward(c)

    wait_bytes(arrived_out.at[pl.ds(0, (peers - 1) * slots)], recv_sem.at[4])

    @pl.loop(0, clusters, unroll=2)
    def _(c):
        spread = jnp.where(wanted_row - c * cluster == node, 1.0, 0.0).astype(BF)
        tile(emb, c)[...] = mm(spread, arrived_out[...]).astype(BF)
        pltpu.make_async_copy(tile(emb, c), tile(og_hbm, c), og_sem).start()

    if reducers == peers:
        wait_bytes(ws.at[pl.ds(0, (peers - 1) * chunk)], recv_sem.at[5])
        wait_bytes(ws.at[pl.ds(0, (peers - 1) * chunk)], send_sem.at[5])
    else:
        @pl.when(me < reducers)
        def _():
            wait_bytes(ws.at[pl.ds(0, (reducers - 1) * chunk)], recv_sem.at[5])

            @pl.loop(1, peers)
            def _(i):
                wait_bytes(ws.at[pl.ds(0, chunk)], send_sem.at[5])

        @pl.when(me >= reducers)
        def _():
            wait_bytes(ws, recv_sem.at[5])

    halves = ws[...].astype(F32).reshape(reducers, 2, part, lanes)
    joined = jnp.concatenate([halves[:, 0], halves[:, 1]], axis=-1)
    wg_out[...] = joined.reshape(width, width)
    wait_bytes(bs.at[pl.ds(0, peers - 1)], recv_sem.at[6])
    wait_bytes(bs.at[pl.ds(0, peers - 1)], send_sem.at[6])
    bg_out[...] = jnp.sum(bs[...], axis=0) * norm
    wait_bytes(rq_send.at[pl.ds(0, peers - 1)], send_sem.at[0])
    wait_bytes(e_send.at[pl.ds(0, (peers - 1) * slots)], send_sem.at[1])
    wait_bytes(g_send.at[pl.ds(0, (peers - 1) * slots)], send_sem.at[2])
    wait_bytes(rs_recv.at[pl.ds(0, (peers - 1) * chunk)], send_sem.at[3])
    wait_bytes(m_send.at[pl.ds(0, (peers - 1) * slots)], send_sem.at[4])
    wait_bytes(ig, out_sem)
    wait_bytes(emb, og_sem)


def pass_kernel(wg_ref, bg_ref, ig_ref, og_ref, ig_out, og_out, wg_out, bg_out):
    @pl.when(pl.program_id(0) == 0)
    def _():
        wg_out[...] = wg_ref[...]
        bg_out[...] = bg_ref[0]

    ig_out[...] = ig_ref[...]
    og_out[...] = og_ref[...]


def on_device(
    node_feats, adj_tiles, live_clusters, req_rows, req_count, req_target, req_weight,
    hist_emb, hist_grad, layer_weight, layer_bias, cotangent,
):
    nodes_dev, width = node_feats.shape
    cluster = adj_tiles.shape[1]
    clusters = nodes_dev // cluster
    peers, slots = req_rows.shape[1:]
    members = lax.axis_size("inner")
    total = peers * slots
    reducers = min(peers, 32)
    part = width // reducers
    chunk, lanes = 2 * part, width // 2
    flip = lambda a: jnp.transpose(a[0])
    vmem = pl.BlockSpec(memory_space=pltpu.VMEM)
    hbm = pl.BlockSpec(memory_space=pl.ANY)
    sds = jax.ShapeDtypeStruct
    full = (nodes_dev, width)
    wg, bg, ig, og = pl.pallas_call(
        functools.partial(main_kernel, members, peers, reducers),
        out_shape=(
            sds((width, width), F32),
            sds((1, width), F32),
            sds(full, BF),
            sds(full, BF),
        ),
        in_specs=[pl.BlockSpec(memory_space=pltpu.SMEM)] + [vmem] * 6 + [hbm] * 5,
        out_specs=(vmem, vmem, hbm, hbm),
        scratch_shapes=[
            pltpu.VMEM(full, BF),
            pltpu.VMEM((nodes_dev, cluster), BF),
            pltpu.VMEM(full, BF),
            pltpu.VMEM(full, BF),
            pltpu.VMEM(full, BF),
            pltpu.VMEM(full, F32),
            pltpu.VMEM(full, BF),
            pltpu.VMEM(full, BF),
            pltpu.VMEM((peers, 1, 128), F32),
            pltpu.VMEM((peers, 1, 128), F32),
            pltpu.VMEM((total, width), BF),
            pltpu.VMEM((total, width), BF),
            pltpu.VMEM((total, width), BF),
            pltpu.VMEM((total, width), BF),
            pltpu.VMEM((total, width), BF),
            pltpu.VMEM((reducers * chunk, lanes), BF),
            pltpu.VMEM((peers * chunk, lanes), BF),
            pltpu.VMEM((reducers * chunk, lanes), BF),
            pltpu.VMEM((peers, 1, width), F32),
            pltpu.VMEM((total, width), BF),
            pltpu.VMEM((total, width), F32),
            pltpu.VMEM((total, width), F32),
            pltpu.VMEM((width, width), F32),
            pltpu.VMEM((8, width), F32),
            pltpu.SemaphoreType.DMA((4,)),
            pltpu.SemaphoreType.DMA((clusters,)),
            pltpu.SemaphoreType.DMA,
            pltpu.SemaphoreType.DMA,
            pltpu.SemaphoreType.DMA((7,)),
            pltpu.SemaphoreType.DMA((7,)),
        ],
        compiler_params=pltpu.CompilerParams(
            collective_id=0, has_side_effects=True, vmem_limit_bytes=58 * 1024 * 1024
        ),
    )(
        live_clusters, flip(req_rows), req_count, flip(req_target), flip(req_weight),
        layer_weight, layer_bias[None, :],
        node_feats, adj_tiles, cotangent, hist_emb, hist_grad,
    )
    whole = lambda a: pl.BlockSpec(a.shape, lambda i: (0,) * len(a.shape))
    per_step = 3 if clusters % 3 == 0 else 1
    tiles = pl.BlockSpec((per_step * cluster, width), lambda i: (i, 0))
    bias_out = sds((width,), F32)
    input_grad, owner_grad, weight_grad, bias_grad = pl.pallas_call(
        pass_kernel,
        grid=(clusters // per_step,),
        out_shape=(sds(full, BF), sds(full, BF), sds(wg.shape, F32), bias_out),
        in_specs=[whole(wg), whole(bg), tiles, tiles],
        out_specs=(tiles, tiles, whole(wg), whole(bias_out)),
        compiler_params=pltpu.CompilerParams(vmem_limit_bytes=60 * 1024 * 1024),
    )(wg, bg, ig, og)
    return input_grad, weight_grad, bias_grad, owner_grad


def solution(mesh):
    both = ("group", "inner")
    return jax.shard_map(
        on_device,
        mesh=mesh,
        in_specs=(
            P(both, None), P(both, None), P(both), P(both, None, None), P(both, None),
            P(both, None, None), P(both, None, None), P(both, None), P(both, None),
            P(), P(), P(both, None),
        ),
        out_specs=(P(both, None), P(), P(), P(both, None)),
        check_vma=False,
    )
```
